256 devices in a mesh: rep: 4 (over z_lo, core), fsdp: 64 (over x, z_hi, y).
Axes of the slice: x: 4, y: 4, z: 8 (z_hi: 4, z_lo: 2; z = z_hi * 2 + z_lo), core: 2. Of those that a mesh axis runs over, the one named last changes fastest.
Arguments:
- activations: bfloat16 [4, 3072, 4096], P('rep', 'fsdp'), may hold values from -6 to 6
- cotangent: bfloat16 [4, 14336, 3072], P('rep', 'fsdp'), may hold values from -6 to 6
- weight: bfloat16 [14336, 4096], P('fsdp', 'rep'), may hold values from -6 to 6
- first_moment: bfloat16 [4, 14336, 4096], P('rep', 'fsdp'), may hold values from -3 to 3
- second_moment: bfloat16 [4, 14336, 4096], P('rep', 'fsdp'), may hold values from 0.099609375 to 10
- momentum: float32 [14336, 4096], P('fsdp', 'rep'), may hold values from -2 to 2
- exponents: int32 [4, 14336, 32], P('rep', 'fsdp'), may hold values from -10 to -7
Outputs:
- new_weight: bfloat16 [14336, 4096], P('fsdp', 'rep')
- new_momentum: float32 [14336, 4096], P('fsdp', 'rep')
- new_first: bfloat16 [4, 14336, 4096], P('rep', 'fsdp')
- new_second: bfloat16 [4, 14336, 4096], P('rep', 'fsdp')
The draws below stay inside these ranges and needn't reach their ends.
All inputs are finite; a program needn't handle non-finite values.
Results may differ from the reference program's by a relative error of at most 0.0039.
Values may be sent and summed in bfloat16 or wider, within the bound.
A program may use at most 128 MiB of HBM per device.

```python
import math
import jax
import jax.numpy as jnp
from jax import lax

D = 4096
F = 14336
BLOCK = 128
REPS = 4
TOKENS = 3072


def plant(drawn, stream_key, least, high):
    place = [jax.random.randint(jax.random.fold_in(stream_key, axis), (), 0, length) for axis, length in enumerate(drawn.shape)]
    main_axis = drawn.shape.index(max(drawn.shape))
    beside = place[:main_axis] + [(place[main_axis] + 1) % drawn.shape[main_axis]] + place[main_axis + 1:]
    return drawn.at[tuple(place)].set(least).at[tuple(beside)].set(high)


def levels(stream_key, extent, cuts, smallest, top_value):
    loudness = 1.0
    for position, blocks in cuts:
        draws = jax.random.uniform(jax.random.fold_in(jax.random.fold_in(stream_key, 6), position), (blocks,), jnp.float32, smallest / len(cuts), top_value / len(cuts))
        loudness = loudness * jnp.repeat(jnp.exp(draws), extent[position] // blocks).reshape((-1,) + (1,) * (len(extent) - 1 - position))
    return loudness


def bell_draw(rng, dims, scale, limit, cuts=(), dtype=jnp.bfloat16):
    entries = jax.random.normal(rng, dims, jnp.float32) * scale
    if len(cuts) > 0:
        entries = levels(rng, dims, cuts, -0.22, 0.18) * entries
    return jnp.clip(entries, min=-limit, max=limit).astype(dtype)


def setup_inputs(seed: int = 0) -> dict:
    streams_of = jax.random.split(jax.random.key(seed), 8)
    activations = bell_draw(streams_of[0], (REPS, TOKENS, D), 1.0, 6.0, ((0, 4), (1, 64)))
    cotangent = bell_draw(streams_of[1], (REPS, F, TOKENS), 1.0, 6.0, ((0, 4), (1, 64)))
    weight = bell_draw(streams_of[2], (F, D), 1.0, 6.0, ((0, 64), (1, 4)))
    first_moment = bell_draw(streams_of[3], (REPS, F, D), 0.5, 3.0, ((0, 4), (1, 64)))
    second_moment = jnp.clip(jnp.exp(math.log(10.0) - 4.609084 * jax.random.uniform(streams_of[4], (REPS, F, D), jnp.float32) ** levels(streams_of[4], (REPS, F, D), ((0, 4), (1, 64)), -0.2, 0.2)), 0.099609375, 10.0).astype(jnp.bfloat16)
    momentum = bell_draw(streams_of[5], (F, D), 0.3, 2.0, ((0, 64), (1, 4)), jnp.float32)
    exponents = plant(jax.random.randint(streams_of[6], (REPS, F, D // BLOCK), -10, -6), jax.random.fold_in(streams_of[6], 1), -10, (-6) - 1).astype(jnp.int32)
    return dict(activations=activations, cotangent=cotangent, weight=weight, first_moment=first_moment, second_moment=second_moment, momentum=momentum, exponents=exponents)


beta_first = 0.9
beta_second = 0.95
inner_rate = 0.25
decay_rate = 0.1
epsilon = 1e-08
clip_limit = 448.0
outer_rate = 0.7
outer_beta = 0.9

def reference(activations, cotangent, weight, first_moment, second_moment, momentum, exponents):
    factor = 1.0 / jnp.sqrt(jnp.float32(D))
    weight_f = weight.astype(jnp.float32)

    def replica(total, items):
        tokens, cot_local, first_old, second_old, expo_local = items
        gradient = jnp.dot(cot_local, tokens, preferred_element_type=jnp.float32) * factor
        first_new = (beta_first * first_old.astype(jnp.float32) + (1.0 - beta_first) * gradient).astype(jnp.bfloat16)
        second_new = (beta_second * second_old.astype(jnp.float32) + (1.0 - beta_second) * gradient * gradient).astype(jnp.bfloat16)
        step_size = inner_rate * (first_new.astype(jnp.float32) / (jnp.sqrt(second_new.astype(jnp.float32)) + epsilon) + decay_rate * weight_f)
        exponent_f = expo_local.astype(jnp.float32)
        shaped = step_size.reshape(F, D // BLOCK, BLOCK) * jnp.exp2(-exponent_f)[:, :, None]
        quantized = jnp.clip(shaped, -clip_limit, clip_limit).astype(jnp.bfloat16)
        restored = quantized.astype(jnp.float32) * jnp.exp2(exponent_f)[:, :, None]
        return (total + restored.reshape(F, D), (first_new, second_new))
    initial = jnp.zeros((F, D), jnp.float32)
    total, outputs = lax.scan(replica, initial, (activations, cotangent, first_moment, second_moment, exponents))
    new_first, new_second = outputs
    pseudo_grad = total / REPS
    new_momentum = outer_beta * momentum + pseudo_grad
    new_weight = (weight_f - outer_rate * (pseudo_grad + outer_beta * new_momentum)).astype(jnp.bfloat16)
    return (new_weight, new_momentum, new_first, new_second)
```

```python
import functools
import math

import jax
import jax.numpy as jnp
from jax import lax
from jax.experimental import pallas as pl
from jax.experimental.pallas import tpu as pltpu
from jax.sharding import PartitionSpec as P

beta_first = 0.9
beta_second = 0.95
inner_rate = 0.25
decay_rate = 0.1
epsilon = 1e-08
clip_limit = 448.0
outer_rate = 0.7
outer_beta = 0.9

MESH = pl.DeviceIdType.MESH
CHUNKS = 4
TILE = 32


def kernel(
    act, cot, wgt, first, second, mom, expo,
    out_weight, out_mom, out_first, out_second,
    cbuf, abuf, fbuf, sbuf, wbuf, mbuf, nfbuf, nsbuf, nwbuf, nmbuf,
    gsend, grecv, usend, urecv, ebuf, limbuf,
    load_sem, own_sem, out_sem,
    cs_sem, cr_sem, as_sem, ar_sem, zs_sem, zr_sem, bs_sem, br_sem,
    gs_sem, gr_sem, us_sem, ur_sem, es_sem, er_sem,
):
    rows, width = first.shape
    count = act.shape[0]
    quarter = width // 4
    cols = quarter // CHUNKS
    half = rows // 2
    factor = 1.0 / math.sqrt(width)

    rep = lax.axis_index("rep")
    place = lax.axis_index("fsdp")
    c = rep % 2
    x, z, y = place // 16, (place // 4) % 4, place % 4
    a = y * (1 - c) + x * c
    b = x * (1 - c) + y * c

    def device(a_, b_, z_):
        return (rep, (b_ * (1 - c) + a_ * c) * 16 + z_ * 4 + a_ * (1 - c) + b_ * c)

    def off(i, d):
        return (i + d + 4) % 4

    a_dev = {d: device(off(a, d), b, z) for d in (1, 2, 3)}
    b_dev = {d: device(a, off(b, d), z) for d in (1, 3)}
    z_dev = {d: device(a, b, off(z, d)) for d in (1, 3)}
    r_dev = {d: (off(rep, d), place) for d in (1, 2, 3)}

    barrier = pltpu.get_barrier_semaphore()
    partners = [*a_dev.values(), *b_dev.values(), *z_dev.values(), *r_dev.values()]
    for dev in partners:
        pl.semaphore_signal(barrier, inc=1, device_id=dev, device_id_type=MESH)

    loads = [
        pltpu.make_async_copy(src, dst, load_sem.at[i])
        for i, (src, dst) in enumerate(
            ((cot, cbuf.at[0]), (first, fbuf), (second, sbuf), (wgt, wbuf), (mom, mbuf), (expo_own(expo, rep), ebuf.at[rep]))
        )
    ]

    def unit(j, a_, b_, z_):
        return abuf.at[j, b_ * (1 - c) + a_ * c, z_, a_ * (1 - c) + b_ * c]

    own = [
        pltpu.make_async_copy(
            act.at[:, pl.ds(pl.multiple_of(a * quarter + j * cols, cols), cols)], unit(j, a, b, z), own_sem.at[j]
        )
        for j in range(CHUNKS)
    ]
    for copy in own + loads:
        copy.start()

    pl.semaphore_wait(barrier, len(partners))

    pending = []

    def remote(src, dst, send, recv, dev):
        copy = pltpu.make_async_remote_copy(
            src_ref=src, dst_ref=dst, send_sem=send, recv_sem=recv, device_id=dev, device_id_type=MESH
        )
        return copy

    def send(*args):
        copy = remote(*args)
        copy.start()
        pending.append(copy)

    def arrived(dst, recv):
        remote(dst, dst, recv, recv, a_dev[1]).wait_recv()

    for j in range(CHUNKS):
        for d in (2, 1, 3):
            send(
                act.at[:, pl.ds(pl.multiple_of(off(a, d) * quarter + j * cols, cols), cols)],
                unit(j, a, b, z), as_sem.at[j, d - 1], ar_sem.at[j, d - 1], a_dev[d],
            )
    halves = (pl.ds(0, half), pl.ds(half, half))
    for i, (to, slot, h) in enumerate(((1, 1, 0), (3, 3, 1), (1, 1, 1), (3, 3, 0))):
        send(cot.at[halves[h]], cbuf.at[slot, halves[h]], cs_sem.at[i], cr_sem.at[i], a_dev[to])
    for d in (1, 2, 3):
        send(expo_own(expo, off(rep, d)), ebuf.at[rep], es_sem.at[d - 1], er_sem.at[d - 1], r_dev[d])

    def block(j, b_, z_, role):
        return abuf.at[j, b_, z_] if role == 0 else abuf.at[j, :, z_, b_]

    def send_block(j, b_, z_, ssem, rsem, dev):
        for role in (0, 1):
            @pl.when(c == role)
            def _(role=role):
                ref = block(j, b_, z_, role)
                remote(ref, ref, ssem, rsem, dev).start()
        pending.append(remote(block(j, b_, z_, 0), block(j, b_, z_, 0), ssem, rsem, dev))

    def block_arrived(j, b_, z_, rsem):
        for role in (0, 1):
            @pl.when(c == role)
            def _(role=role):
                arrived(block(j, b_, z_, role), rsem)

    for j in range(CHUNKS):
        own[j].wait()
        for d in (1, 2, 3):
            arrived(unit(j, off(a, -d), b, z), ar_sem.at[j, d - 1])
        send_block(j, b, z, zs_sem.at[j, 0], zr_sem.at[j, 0], z_dev[1])
        send_block(j, b, z, zs_sem.at[j, 1], zr_sem.at[j, 1], z_dev[3])

    def z_two(j):
        block_arrived(j, b, off(z, -1), zr_sem.at[j, 0])
        block_arrived(j, b, off(z, 1), zr_sem.at[j, 1])
        if j % 2 == 0:
            send_block(j, b, off(z, -1), zs_sem.at[j, 2], zr_sem.at[j, 2], z_dev[1])
        else:
            send_block(j, b, off(z, 1), zs_sem.at[j, 2], zr_sem.at[j, 2], z_dev[3])

    def z_three(j):
        block_arrived(j, b, off(z, 2), zr_sem.at[j, 2])

    z_two(0)
    z_two(1)
    arrived(cbuf.at[1, halves[0]], cr_sem.at[0])
    send(cbuf.at[1, halves[0]], cbuf.at[2, halves[0]], cs_sem.at[4], cr_sem.at[4], a_dev[1])
    arrived(cbuf.at[3, halves[1]], cr_sem.at[1])
    send(cbuf.at[3, halves[1]], cbuf.at[2, halves[1]], cs_sem.at[5], cr_sem.at[5], a_dev[3])
    z_two(2)
    z_two(3)
    arrived(cbuf.at[1, halves[1]], cr_sem.at[2])
    arrived(cbuf.at[3, halves[0]], cr_sem.at[3])

    plane = [z, off(z, -1), off(z, 1), off(z, 2)]

    def b_one(j):
        z_three(j)
        for k in range(4):
            send_block(j, b, plane[k], bs_sem.at[j, 0, k], br_sem.at[j, 0, k], b_dev[1])
            send_block(j, b, plane[k], bs_sem.at[j, 1, k], br_sem.at[j, 1, k], b_dev[3])

    def b_two(j):
        for k in range(4):
            block_arrived(j, off(b, -1), plane[k], br_sem.at[j, 0, k])
            if k in (0, 3):
                send_block(j, off(b, -1), plane[k], bs_sem.at[j, 2, k], br_sem.at[j, 2, k], b_dev[1])
            block_arrived(j, off(b, 1), plane[k], br_sem.at[j, 1, k])
            if k in (1, 2):
                send_block(j, off(b, 1), plane[k], bs_sem.at[j, 2, k], br_sem.at[j, 2, k], b_dev[3])

    def b_three(j):
        for k in range(4):
            block_arrived(j, off(b, 2), plane[k], br_sem.at[j, 2, k])

    tokens = 64 * count

    def product(j):
        def one(i, carry):
            s = (i + 2) % 4
            got = jnp.dot(cbuf[s], abuf[j].reshape(tokens, cols), preferred_element_type=jnp.float32)
            gsend[j, s] = (got * factor).astype(jnp.bfloat16)

            @pl.when(s > 0)
            def _():
                remote(
                    gsend.at[j, s], grecv.at[j, a], gs_sem.at[j, s], gr_sem.at[j, s],
                    device(off(a, -s), b, z),
                ).start()

            return carry

        lax.fori_loop(0, 4, one, 0)
        for s in (1, 2, 3):
            pending.append(remote(gsend.at[j, s], grecv.at[j, a], gs_sem.at[j, s], gr_sem.at[j, s], a_dev[1]))
        grecv[j, a] = gsend[j, 0]

    def inner(j):
        for s in (1, 2, 3):
            arrived(grecv.at[j, off(a, s)], gr_sem.at[j, s])

        def one(i, carry):
            span = pl.ds(pl.multiple_of(i * TILE, TILE), TILE)
            for q in range(4):
                where = pl.ds(q * quarter + j * cols, cols)
                gradient = grecv[j, q, span].astype(jnp.float32)
                new_first = (
                    beta_first * fbuf[span, where].astype(jnp.float32) + (1.0 - beta_first) * gradient
                ).astype(jnp.bfloat16)
                new_second = (
                    beta_second * sbuf[span, where].astype(jnp.float32)
                    + (1.0 - beta_second) * gradient * gradient
                ).astype(jnp.bfloat16)
                nfbuf[span, where] = new_first
                nsbuf[span, where] = new_second
                ratio = new_first.astype(jnp.float32) / (jnp.sqrt(new_second.astype(jnp.float32)) + epsilon)
                usend[j, q, span] = ratio.astype(jnp.bfloat16)
            urecv[j, rep, span] = usend[j, rep, span]
            return carry

        lax.fori_loop(0, rows // TILE, one, 0)
        for d in (2, 3, 1):
            send(usend.at[j, off(rep, d)], urecv.at[j, rep], us_sem.at[j, d - 1], ur_sem.at[j, d - 1], r_dev[d])

    def outer(j):
        blocks = ebuf.shape[1]
        span_of = lax.broadcasted_iota(jnp.int32, (blocks, cols), 1) // (quarter // blocks) + j * (cols * blocks // quarter)
        spread = (span_of == lax.broadcasted_iota(jnp.int32, (blocks, cols), 0)).astype(jnp.float32).astype(jnp.bfloat16)
        for r in range(4):
            limits = (clip_limit * jnp.exp2(ebuf[r].astype(jnp.float32))).astype(jnp.bfloat16)
            limbuf[r] = lax.dot_general(
                limits, spread, (((0,), (0,)), ((), ())), preferred_element_type=jnp.float32
            )
        for d in (1, 2, 3):
            arrived(urecv.at[j, off(rep, -d)], ur_sem.at[j, d - 1])

        def one(i, carry):
            span = pl.ds(pl.multiple_of(i * TILE, TILE), TILE)
            where = pl.ds(j * cols, cols)
            weight = wbuf[span, where].astype(jnp.float32)
            total = jnp.zeros_like(weight)
            for r in range(4):
                delta = inner_rate * (urecv[j, r, span].astype(jnp.float32) + decay_rate * weight)
                limit = limbuf[r, span]
                total = total + jnp.minimum(jnp.maximum(delta, -limit), limit)
            pseudo = total * 0.25
            new_mom = outer_beta * mbuf[span, where] + pseudo
            nmbuf[span, where] = new_mom
            nwbuf[span, where] = (weight - outer_rate * (pseudo + outer_beta * new_mom)).astype(jnp.bfloat16)
            return carry

        lax.fori_loop(0, rows // TILE, one, 0)

    def ready(j):
        if j == 0:
            arrived(cbuf.at[2, halves[0]], cr_sem.at[4])
            arrived(cbuf.at[2, halves[1]], cr_sem.at[5])
            loads[0].wait()
        product(j)

    b_one(0)
    b_one(1)
    b_two(0)
    b_one(2)
    b_two(1)
    b_three(0)
    ready(0)
    b_one(3)
    b_two(2)
    b_three(1)
    ready(1)
    for copy in loads[1:]:
        copy.wait()
    for d in (1, 2, 3):
        arrived(ebuf.at[off(rep, -d)], er_sem.at[d - 1])
    inner(0)
    b_two(3)
    b_three(2)
    ready(2)
    inner(1)
    outer(0)
    b_three(3)
    ready(3)
    inner(2)
    outer(1)
    inner(3)
    outs = [
        pltpu.make_async_copy(nfbuf, out_first, out_sem.at[0]),
        pltpu.make_async_copy(nsbuf, out_second, out_sem.at[1]),
    ]
    for copy in outs:
        copy.start()
    outer(2)
    outer(3)
    last = [
        pltpu.make_async_copy(nwbuf, out_weight, out_sem.at[2]),
        pltpu.make_async_copy(nmbuf, out_mom, out_sem.at[3]),
    ]
    for copy in last:
        copy.start()
    for copy in pending:
        copy.wait_send()
    for copy in outs + last:
        copy.wait()


def expo_own(expo, q):
    blocks = expo.shape[0] // 4
    return expo.at[pl.ds(pl.multiple_of(q * blocks, blocks), blocks)]


def shards(activations, cotangent, weight, first_moment, second_moment, momentum, exponents):
    act, cot, first, second = activations[0], cotangent[0], first_moment[0], second_moment[0]
    expo = exponents[0].T
    rows, width = first.shape
    count, tokens = act.shape[0], cot.shape[1]
    quarter = weight.shape[1]
    cols = quarter // CHUNKS
    bf16, f32 = jnp.bfloat16, jnp.float32
    dma = pltpu.SemaphoreType.DMA
    new_weight, new_mom, new_first, new_second = pl.pallas_call(
        kernel,
        out_shape=(
            jax.ShapeDtypeStruct(weight.shape, bf16),
            jax.ShapeDtypeStruct(momentum.shape, f32),
            jax.ShapeDtypeStruct(first.shape, bf16),
            jax.ShapeDtypeStruct(second.shape, bf16),
        ),
        in_specs=[pl.BlockSpec(memory_space=pl.ANY)] * 7,
        out_specs=(pl.BlockSpec(memory_space=pl.ANY),) * 4,
        scratch_shapes=[
            pltpu.VMEM((4, rows, tokens), bf16),
            pltpu.VMEM((CHUNKS, 4, 4, 4, count, cols), bf16),
            pltpu.VMEM((rows, width), bf16),
            pltpu.VMEM((rows, width), bf16),
            pltpu.VMEM((rows, quarter), bf16),
            pltpu.VMEM((rows, quarter), f32),
            pltpu.VMEM((rows, width), bf16),
            pltpu.VMEM((rows, width), bf16),
            pltpu.VMEM((rows, quarter), bf16),
            pltpu.VMEM((rows, quarter), f32),
            pltpu.VMEM((CHUNKS, 4, rows, cols), bf16),
            pltpu.VMEM((CHUNKS, 4, rows, cols), bf16),
            pltpu.VMEM((CHUNKS, 4, rows, cols), bf16),
            pltpu.VMEM((CHUNKS, 4, rows, cols), bf16),
            pltpu.VMEM((4, expo.shape[0] // 4, rows), jnp.int32),
            pltpu.VMEM((4, rows, cols), f32),
            dma((6,)), dma((CHUNKS,)), dma((4,)),
            dma((6,)), dma((6,)),
            dma((CHUNKS, 3)), dma((CHUNKS, 3)),
            dma((CHUNKS, 3)), dma((CHUNKS, 3)),
            dma((CHUNKS, 3, 4)), dma((CHUNKS, 3, 4)),
            dma((CHUNKS, 4)), dma((CHUNKS, 4)),
            dma((CHUNKS, 3)), dma((CHUNKS, 3)),
            dma((3,)), dma((3,)),
        ],
        compiler_params=pltpu.CompilerParams(
            collective_id=0, has_side_effects=True, vmem_limit_bytes=52 * 1024 * 1024
        ),
        cost_estimate=pl.CostEstimate(flops=2 * rows * tokens * width, bytes_accessed=14_000_000, transcendentals=rows * width),
    )(act, cot, weight, first, second, momentum, expo)
    return (new_weight, new_mom, new_first[None], new_second[None])


def solution(mesh):
    in_specs = (
        P("rep", "fsdp", None),
        P("rep", "fsdp", None),
        P("fsdp", "rep"),
        P("rep", "fsdp", None),
        P("rep", "fsdp", None),
        P("fsdp", "rep"),
        P("rep", "fsdp", None),
    )
    out_specs = (P("fsdp", "rep"), P("fsdp", "rep"), P("rep", "fsdp", None), P("rep", "fsdp", None))
    return jax.shard_map(shards, mesh=mesh, in_specs=in_specs, out_specs=out_specs, check_vma=False)
```

```python
import functools
import math

import jax
import jax.numpy as jnp
from jax import lax
from jax.experimental import pallas as pl
from jax.experimental.pallas import tpu as pltpu
from jax.sharding import PartitionSpec as P

beta_first = 0.9
beta_second = 0.95
inner_rate = 0.25
decay_rate = 0.1
epsilon = 1e-08
clip_limit = 448.0
outer_rate = 0.7
outer_beta = 0.9

MESH = pl.DeviceIdType.MESH
PARTS = (256, 256, 256, 256)
CHUNKS = len(PARTS)
STARTS = tuple(sum(PARTS[:j]) for j in range(CHUNKS))
TILE = 32
SIDES = (0, 1, 1, 0)


def kernel(
    act, cot, wgt, first, second, mom, expo,
    out_weight, out_mom, out_first, out_second,
    cbuf, abuf, fbuf, sbuf, wbuf, mbuf,
    gsend, grecv, usend, urecv, ebuf, limbuf,
    load_sem, own_sem,
    cs_sem, cr_sem, as_sem, ar_sem, zs_sem, zr_sem, bs_sem, br_sem,
    gs_sem, gr_sem, us_sem, ur_sem, es_sem, er_sem,
):
    rows, width = first.shape
    count = act.shape[0]
    quarter = width // 4
    half = rows // 2
    factor = 1.0 / math.sqrt(width)

    rep = lax.axis_index("rep")
    place = lax.axis_index("fsdp")
    c = rep % 2
    x, z, y = place // 16, (place // 4) % 4, place % 4
    a = y * (1 - c) + x * c
    b = x * (1 - c) + y * c

    def device(a_, b_, z_):
        return (rep, (b_ * (1 - c) + a_ * c) * 16 + z_ * 4 + a_ * (1 - c) + b_ * c)

    def off(i, d):
        return (i + d + 4) % 4

    a_dev = {d: device(off(a, d), b, z) for d in (1, 2, 3)}
    b_dev = {d: device(a, off(b, d), z) for d in (1, 3)}
    z_dev = {d: device(a, b, off(z, d)) for d in (1, 3)}
    r_dev = {d: (off(rep, d), place) for d in (1, 2, 3)}

    barrier = pltpu.get_barrier_semaphore()
    partners = [*a_dev.values(), *b_dev.values(), *z_dev.values(), *r_dev.values()]
    for dev in partners:
        pl.semaphore_signal(barrier, inc=1, device_id=dev, device_id_type=MESH)

    loads = [
        pltpu.make_async_copy(src, dst, load_sem.at[i])
        for i, (src, dst) in enumerate(
            ((cot, cbuf.at[0]), (first, fbuf), (second, sbuf), (wgt, wbuf), (mom, mbuf), (expo_own(expo, rep), ebuf.at[rep]))
        )
    ]

    def unit(j, a_, b_, z_):
        return abuf[j].at[b_ * (1 - c) + a_ * c, z_, a_ * (1 - c) + b_ * c]

    own = [
        pltpu.make_async_copy(
            act.at[:, pl.ds(pl.multiple_of(a * quarter + STARTS[j], 128), PARTS[j])], unit(j, a, b, z), own_sem.at[j]
        )
        for j in range(CHUNKS)
    ]
    for copy in own + loads:
        copy.start()

    pl.semaphore_wait(barrier, len(partners))

    pending = []

    def remote(src, dst, send, recv, dev):
        copy = pltpu.make_async_remote_copy(
            src_ref=src, dst_ref=dst, send_sem=send, recv_sem=recv, device_id=dev, device_id_type=MESH
        )
        return copy

    def send(*args):
        copy = remote(*args)
        copy.start()
        pending.append(copy)

    def arrived(dst, recv):
        remote(dst, dst, recv, recv, a_dev[1]).wait_recv()

    def act_out(j):
        for d in (2, 1, 3):
            send(
                act.at[:, pl.ds(pl.multiple_of(off(a, d) * quarter + STARTS[j], 128), PARTS[j])],
                unit(j, a, b, z), as_sem.at[j, d - 1], ar_sem.at[j, d - 1], a_dev[d],
            )

    halves = (pl.ds(0, half), pl.ds(half, half))

    def cot_out(i):
        for k, (to, slot, h) in enumerate((((1, 1, 0), (3, 3, 1)), ((1, 1, 1), (3, 3, 0)))[i]):
            send(cot.at[halves[h]], cbuf.at[slot, halves[h]], cs_sem.at[2 * i + k], cr_sem.at[2 * i + k], a_dev[to])

    for d in (1, 2, 3):
        send(expo_own(expo, off(rep, d)), ebuf.at[rep], es_sem.at[d - 1], er_sem.at[d - 1], r_dev[d])

    def block(j, b_, z_, role):
        return abuf[j].at[b_, z_] if role == 0 else abuf[j].at[:, z_, b_]

    def send_block(j, b_, z_, ssem, rsem, dev):
        for role in (0, 1):
            @pl.when(c == role)
            def _(role=role):
                ref = block(j, b_, z_, role)
                remote(ref, ref, ssem, rsem, dev).start()
        pending.append(remote(block(j, b_, z_, 0), block(j, b_, z_, 0), ssem, rsem, dev))

    def block_arrived(j, b_, z_, rsem):
        for role in (0, 1):
            @pl.when(c == role)
            def _(role=role):
                arrived(block(j, b_, z_, role), rsem)

    def z_one(j):
        own[j].wait()
        for d in (1, 2, 3):
            arrived(unit(j, off(a, -d), b, z), ar_sem.at[j, d - 1])
        send_block(j, b, z, zs_sem.at[j, 0], zr_sem.at[j, 0], z_dev[1])
        send_block(j, b, z, zs_sem.at[j, 1], zr_sem.at[j, 1], z_dev[3])

    def z_two(j):
        d = (-1, 1)[j % 2]
        block_arrived(j, b, off(z, d), zr_sem.at[j, j % 2])
        send_block(j, b, off(z, d), zs_sem.at[j, 2], zr_sem.at[j, 2], z_dev[-d % 4])
        block_arrived(j, b, off(z, -d), zr_sem.at[j, 1 - j % 2])

    def z_three(j):
        block_arrived(j, b, off(z, 2), zr_sem.at[j, 2])

    def cot_one(d):
        slot = (1, 3)[d]
        arrived(cbuf.at[slot, halves[d]], cr_sem.at[d])
        send(cbuf.at[slot, halves[d]], cbuf.at[2, halves[d]], cs_sem.at[4 + d], cr_sem.at[4 + d], a_dev[slot])

    def cot_two():
        arrived(cbuf.at[1, halves[1]], cr_sem.at[2])
        arrived(cbuf.at[3, halves[0]], cr_sem.at[3])

    def cot_three():
        arrived(cbuf.at[2, halves[0]], cr_sem.at[4])
        arrived(cbuf.at[2, halves[1]], cr_sem.at[5])

    plane = [z, off(z, -1), off(z, 1), off(z, 2)]

    def b_one(j, k):
        send_block(j, b, plane[k], bs_sem.at[j, 0, k], br_sem.at[j, 0, k], b_dev[1])
        send_block(j, b, plane[k], bs_sem.at[j, 1, k], br_sem.at[j, 1, k], b_dev[3])

    def b_two(j, k):
        d = SIDES[k]
        block_arrived(j, off(b, 2 * d - 1), plane[k], br_sem.at[j, d, k])
        send_block(j, off(b, 2 * d - 1), plane[k], bs_sem.at[j, 2, k], br_sem.at[j, 2, k], b_dev[1 + 2 * d])

    def b_three(j):
        for k in range(4):
            d = 1 - SIDES[k]
            block_arrived(j, off(b, 2 * d - 1), plane[k], br_sem.at[j, d, k])
            block_arrived(j, off(b, 2), plane[k], br_sem.at[j, 2, k])

    tokens = 64 * count

    def product(j, s):
        got = jnp.dot(cbuf[s], abuf[j][...].reshape(tokens, PARTS[j]), preferred_element_type=jnp.float32)
        got = (got * factor).astype(jnp.bfloat16)
        if s == 0:
            grecv[j][a] = got
        else:
            gsend[j][s] = got
            send(gsend[j].at[s], grecv[j].at[a], gs_sem.at[j, s], gr_sem.at[j, s], a_dev[4 - s])

    def inner(j):
        for s in (1, 2, 3):
            arrived(grecv[j].at[off(a, s)], gr_sem.at[j, s])

        def one(i, carry):
            span = pl.ds(pl.multiple_of(i * TILE, TILE), TILE)
            for q in range(4):
                where = pl.ds(q * quarter + STARTS[j], PARTS[j])
                gradient = grecv[j][q, span].astype(jnp.float32)
                new_first = (
                    beta_first * fbuf[span, where].astype(jnp.float32) + (1.0 - beta_first) * gradient
                ).astype(jnp.bfloat16)
                new_second = (
                    beta_second * sbuf[span, where].astype(jnp.float32)
                    + (1.0 - beta_second) * gradient * gradient
                ).astype(jnp.bfloat16)
                out_first[span, where] = new_first
                out_second[span, where] = new_second
                ratio = new_first.astype(jnp.float32) / (jnp.sqrt(new_second.astype(jnp.float32)) + epsilon)
                usend[j][q, span] = ratio.astype(jnp.bfloat16)
            urecv[j][rep, span] = usend[j][rep, span]
            return carry

        lax.fori_loop(0, rows // TILE, one, 0)
        for d in (2, 3, 1):
            send(usend[j].at[off(rep, d)], urecv[j].at[rep], us_sem.at[j, d - 1], ur_sem.at[j, d - 1], r_dev[d])

    def limits():
        for d in (1, 2, 3):
            arrived(ebuf.at[off(rep, -d)], er_sem.at[d - 1])
        loads[5].wait()
        blocks = ebuf.shape[1]
        span_of = lax.broadcasted_iota(jnp.int32, (blocks, quarter), 1) // (quarter // blocks)
        spread = (span_of == lax.broadcasted_iota(jnp.int32, (blocks, quarter), 0)).astype(jnp.float32).astype(jnp.bfloat16)
        for r in range(4):
            level = (clip_limit * jnp.exp2(ebuf[r].astype(jnp.float32))).astype(jnp.bfloat16)
            limbuf[r] = lax.dot_general(
                level, spread, (((0,), (0,)), ((), ())), preferred_element_type=jnp.float32
            ).astype(jnp.bfloat16)

    def outer(j):
        for d in (1, 2, 3):
            arrived(urecv[j].at[off(rep, -d)], ur_sem.at[j, d - 1])

        def one(i, carry):
            span = pl.ds(pl.multiple_of(i * TILE, TILE), TILE)
            where = pl.ds(STARTS[j], PARTS[j])
            weight = wbuf[span, where].astype(jnp.float32)
            total = jnp.zeros_like(weight)
            for r in range(4):
                delta = inner_rate * (urecv[j][r, span].astype(jnp.float32) + decay_rate * weight)
                limit = limbuf[r, span, where].astype(jnp.float32)
                total = total + jnp.minimum(jnp.maximum(delta, -limit), limit)
            pseudo = total * 0.25
            new_mom = outer_beta * mbuf[span, where] + pseudo
            out_mom[span, where] = new_mom
            out_weight[span, where] = (weight - outer_rate * (pseudo + outer_beta * new_mom)).astype(jnp.bfloat16)
            return carry

        lax.fori_loop(0, rows // TILE, one, 0)

    def moments():
        for copy in loads[1:5]:
            copy.wait()

    act_out(0)
    act_out(1)
    act_out(2)
    act_out(3)
    cot_out(0)
    z_one(1)
    cot_out(1)
    z_one(3)
    z_one(2)
    cot_one(0)
    b_one(3, 0)
    z_two(3)
    b_one(3, 1)
    cot_one(1)
    b_one(3, 2)
    z_two(2)
    z_one(0)
    b_one(2, 2)
    b_one(2, 1)
    limits()
    b_one(2, 0)
    z_three(3)
    cot_two()
    b_two(3, 2)
    b_one(3, 3)
    z_two(1)
    b_two(2, 1)
    z_three(2)
    b_one(1, 1)
    b_two(3, 0)
    b_one(2, 3)
    b_two(3, 1)
    b_two(2, 2)
    b_two(3, 3)
    b_one(1, 2)
    z_two(0)
    b_two(2, 0)
    b_one(0, 2)
    b_one(1, 0)
    b_three(3)
    b_one(0, 1)
    loads[0].wait()
    product(3, 1)
    z_three(1)
    cot_three()
    b_two(1, 1)
    b_one(1, 3)
    b_two(2, 3)
    product(3, 0)
    product(3, 3)
    b_two(1, 2)
    z_three(0)
    b_two(1, 0)
    product(3, 2)
    b_one(0, 3)
    b_two(1, 3)
    b_one(0, 0)
    b_three(2)
    product(2, 3)
    product(2, 0)
    product(2, 1)
    b_two(0, 2)
    product(2, 2)
    moments()
    inner(3)
    b_two(0, 1)
    b_three(1)
    b_two(0, 3)
    product(1, 3)
    product(1, 0)
    b_two(0, 0)
    product(1, 2)
    product(1, 1)
    inner(2)
    b_three(0)
    product(0, 3)
    product(0, 1)
    product(0, 2)
    inner(1)
    product(0, 0)
    outer(3)
    outer(2)
    inner(0)
    outer(1)
    outer(0)
    for copy in pending:
        copy.wait_send()


def flush(*refs):
    count = (len(refs) - 1) // 2
    sem = refs[-1]
    copies = [pltpu.make_async_copy(refs[i], refs[count + i], sem.at[i]) for i in range(count)]
    for copy in copies:
        copy.start()
    for copy in copies:
        copy.wait()


def expo_own(expo, q):
    blocks = expo.shape[0] // 4
    return expo.at[pl.ds(pl.multiple_of(q * blocks, blocks), blocks)]


def shards(activations, cotangent, weight, first_moment, second_moment, momentum, exponents):
    act, cot, first, second = activations[0], cotangent[0], first_moment[0], second_moment[0]
    expo = exponents[0].T
    rows, width = first.shape
    count, tokens = act.shape[0], cot.shape[1]
    quarter = weight.shape[1]
    bf16, f32 = jnp.bfloat16, jnp.float32
    dma = pltpu.SemaphoreType.DMA
    results = (
        (weight.shape, bf16),
        (momentum.shape, f32),
        (first.shape, bf16),
        (second.shape, bf16),
    )
    pieces = [pltpu.VMEM((4, rows, part), bf16) for part in PARTS]
    held = pl.pallas_call(
        kernel,
        out_shape=tuple(pltpu.VMEM(*r) for r in results),
        in_specs=[pl.BlockSpec(memory_space=pltpu.HBM)] * 7,
        out_specs=(pl.BlockSpec(memory_space=pltpu.VMEM),) * 4,
        scratch_shapes=[
            pltpu.VMEM((4, rows, tokens), bf16),
            [pltpu.VMEM((4, 4, 4, count, part), bf16) for part in PARTS],
            pltpu.VMEM((rows, width), bf16),
            pltpu.VMEM((rows, width), bf16),
            pltpu.VMEM((rows, quarter), bf16),
            pltpu.VMEM((rows, quarter), f32),
            pieces, pieces, pieces, pieces,
            pltpu.VMEM((4, expo.shape[0] // 4, rows), jnp.int32),
            pltpu.VMEM((4, rows, quarter), bf16),
            dma((6,)), dma((CHUNKS,)),
            dma((6,)), dma((6,)),
            dma((CHUNKS, 3)), dma((CHUNKS, 3)),
            dma((CHUNKS, 3)), dma((CHUNKS, 3)),
            dma((CHUNKS, 3, 4)), dma((CHUNKS, 3, 4)),
            dma((CHUNKS, 4)), dma((CHUNKS, 4)),
            dma((CHUNKS, 3)), dma((CHUNKS, 3)),
            dma((3,)), dma((3,)),
        ],
        compiler_params=pltpu.CompilerParams(
            collective_id=0, has_side_effects=True, vmem_limit_bytes=40 * 1024 * 1024
        ),
        cost_estimate=pl.CostEstimate(
            flops=2 * rows * tokens * width, bytes_accessed=14_000_000, transcendentals=rows * width
        ),
    )(*(pltpu.with_memory_space_constraint(v, pltpu.HBM) for v in (act, cot, weight, first, second, momentum, expo)))
    new_weight, new_mom, new_first, new_second = pl.pallas_call(
        flush,
        out_shape=tuple(jax.ShapeDtypeStruct(*r) for r in results),
        in_specs=[pl.BlockSpec(memory_space=pltpu.VMEM)] * 4,
        out_specs=(pl.BlockSpec(memory_space=pltpu.HBM),) * 4,
        scratch_shapes=[dma((4,))],
        compiler_params=pltpu.CompilerParams(vmem_limit_bytes=2 * 1024 * 1024),
    )(*(pltpu.with_memory_space_constraint(v, pltpu.VMEM) for v in held))
    return (new_weight, new_mom, new_first[None], new_second[None])


def solution(mesh):
    in_specs = (
        P("rep", "fsdp", None),
        P("rep", "fsdp", None),
        P("fsdp", "rep"),
        P("rep", "fsdp", None),
        P("rep", "fsdp", None),
        P("fsdp", "rep"),
        P("rep", "fsdp", None),
    )
    out_specs = (P("fsdp", "rep"), P("fsdp", "rep"), P("rep", "fsdp", None), P("rep", "fsdp", None))
    return jax.shard_map(shards, mesh=mesh, in_specs=in_specs, out_specs=out_specs, check_vma=False)
```

```python
import functools
import math

import jax
import jax.numpy as jnp
from jax import lax
from jax.experimental import pallas as pl
from jax.experimental.pallas import tpu as pltpu
from jax.sharding import PartitionSpec as P

beta_first = 0.9
beta_second = 0.95
inner_rate = 0.25
decay_rate = 0.1
epsilon = 1e-08
clip_limit = 448.0
outer_rate = 0.7
outer_beta = 0.9

MESH = pl.DeviceIdType.MESH
PARTS = (256, 256, 256, 256)
CHUNKS = len(PARTS)
STARTS = tuple(sum(PARTS[:j]) for j in range(CHUNKS))
TILE = 32
SIDES = (0, 1, 1, 0)


def kernel(
    act, cot, wgt, first, second, mom, expo,
    out_weight, out_mom, out_first, out_second,
    cbuf, abuf, fbuf, sbuf, wbuf, mbuf,
    gsend, grecv, usend, urecv, ebuf, limbuf,
    load_sem, own_sem,
    cs_sem, cr_sem, as_sem, ar_sem, zs_sem, zr_sem, bs_sem, br_sem,
    gs_sem, gr_sem, us_sem, ur_sem, es_sem, er_sem,
):
    rows, width = first.shape
    count = act.shape[0]
    quarter = width // 4
    half = rows // 2
    factor = 1.0 / math.sqrt(width)

    rep = lax.axis_index("rep")
    place = lax.axis_index("fsdp")
    c = rep % 2
    x, z, y = place // 16, (place // 4) % 4, place % 4
    a = y * (1 - c) + x * c
    b = x * (1 - c) + y * c

    def device(a_, b_, z_):
        return (rep, (b_ * (1 - c) + a_ * c) * 16 + z_ * 4 + a_ * (1 - c) + b_ * c)

    def off(i, d):
        return (i + d + 4) % 4

    a_dev = {d: device(off(a, d), b, z) for d in (1, 2, 3)}
    b_dev = {d: device(a, off(b, d), z) for d in (1, 3)}
    z_dev = {d: device(a, b, off(z, d)) for d in (1, 3)}
    r_dev = {d: (off(rep, d), place) for d in (1, 2, 3)}

    barrier = pltpu.get_barrier_semaphore()
    partners = [*a_dev.values(), *b_dev.values(), *z_dev.values(), *r_dev.values()]
    for dev in partners:
        pl.semaphore_signal(barrier, inc=1, device_id=dev, device_id_type=MESH)

    loads = [
        pltpu.make_async_copy(src, dst, load_sem.at[i])
        for i, (src, dst) in enumerate(
            ((cot, cbuf.at[0]), (first, fbuf), (second, sbuf), (wgt, wbuf), (mom, mbuf), (expo_own(expo, rep), ebuf.at[rep]))
        )
    ]

    def unit(j, a_, b_, z_):
        return abuf[j].at[b_, z_, a_]

    own = [
        pltpu.make_async_copy(
            act.at[:, pl.ds(pl.multiple_of(a * quarter + STARTS[j], 128), PARTS[j])], unit(j, a, b, z), own_sem.at[j]
        )
        for j in range(CHUNKS)
    ]
    for copy in own + loads:
        copy.start()

    pl.semaphore_wait(barrier, len(partners))

    pending = []

    def remote(src, dst, send, recv, dev):
        copy = pltpu.make_async_remote_copy(
            src_ref=src, dst_ref=dst, send_sem=send, recv_sem=recv, device_id=dev, device_id_type=MESH
        )
        return copy

    def send(*args):
        copy = remote(*args)
        copy.start()
        pending.append(copy)

    def arrived(dst, recv):
        remote(dst, dst, recv, recv, a_dev[1]).wait_recv()

    def act_out(j):
        for d in (2, 1, 3):
            send(
                act.at[:, pl.ds(pl.multiple_of(off(a, d) * quarter + STARTS[j], 128), PARTS[j])],
                unit(j, a, b, z), as_sem.at[j, d - 1], ar_sem.at[j, d - 1], a_dev[d],
            )

    halves = (pl.ds(0, half), pl.ds(half, half))

    def cot_out(i):
        for k, (to, slot, h) in enumerate((((1, 1, 0), (3, 3, 1)), ((1, 1, 1), (3, 3, 0)))[i]):
            send(cot.at[halves[h]], cbuf.at[slot, halves[h]], cs_sem.at[2 * i + k], cr_sem.at[2 * i + k], a_dev[to])

    for d in (1, 2, 3):
        send(expo_own(expo, off(rep, d)), ebuf.at[rep], es_sem.at[d - 1], er_sem.at[d - 1], r_dev[d])

    def send_block(j, b_, z_, ssem, rsem, dev):
        send(abuf[j].at[b_, z_], abuf[j].at[b_, z_], ssem, rsem, dev)

    def block_arrived(j, b_, z_, rsem):
        arrived(abuf[j].at[b_, z_], rsem)

    def z_one(j):
        own[j].wait()
        for d in (1, 2, 3):
            arrived(unit(j, off(a, -d), b, z), ar_sem.at[j, d - 1])
        send_block(j, b, z, zs_sem.at[j, 0], zr_sem.at[j, 0], z_dev[1])
        send_block(j, b, z, zs_sem.at[j, 1], zr_sem.at[j, 1], z_dev[3])

    def z_two(j):
        d = (-1, 1)[j % 2]
        block_arrived(j, b, off(z, d), zr_sem.at[j, j % 2])
        send_block(j, b, off(z, d), zs_sem.at[j, 2], zr_sem.at[j, 2], z_dev[-d % 4])
        block_arrived(j, b, off(z, -d), zr_sem.at[j, 1 - j % 2])

    def z_three(j):
        block_arrived(j, b, off(z, 2), zr_sem.at[j, 2])

    def cot_one(d):
        slot = (1, 3)[d]
        arrived(cbuf.at[slot, halves[d]], cr_sem.at[d])
        send(cbuf.at[slot, halves[d]], cbuf.at[2, halves[d]], cs_sem.at[4 + d], cr_sem.at[4 + d], a_dev[slot])

    def cot_two():
        arrived(cbuf.at[1, halves[1]], cr_sem.at[2])
        arrived(cbuf.at[3, halves[0]], cr_sem.at[3])

    def cot_three():
        arrived(cbuf.at[2, halves[0]], cr_sem.at[4])
        arrived(cbuf.at[2, halves[1]], cr_sem.at[5])

    plane = [z, off(z, -1), off(z, 1), off(z, 2)]

    def b_one(j, k):
        send_block(j, b, plane[k], bs_sem.at[j, 0, k], br_sem.at[j, 0, k], b_dev[1])
        send_block(j, b, plane[k], bs_sem.at[j, 1, k], br_sem.at[j, 1, k], b_dev[3])

    def b_two(j, k):
        d = SIDES[k]
        block_arrived(j, off(b, 2 * d - 1), plane[k], br_sem.at[j, d, k])
        send_block(j, off(b, 2 * d - 1), plane[k], bs_sem.at[j, 2, k], br_sem.at[j, 2, k], b_dev[1 + 2 * d])

    def b_three(j):
        for k in range(4):
            d = 1 - SIDES[k]
            block_arrived(j, off(b, 2 * d - 1), plane[k], br_sem.at[j, d, k])
            block_arrived(j, off(b, 2), plane[k], br_sem.at[j, 2, k])

    group = 16 * count

    def product(j, s):
        def one(p, total):
            held = [abuf[j][p * (1 - c) + q * c, k, q * (1 - c) + p * c] for k in range(4) for q in range(4)]
            mine = cbuf[s, :, pl.ds(pl.multiple_of(p * group, 128), group)]
            return total + jnp.dot(mine, jnp.concatenate(held, axis=0), preferred_element_type=jnp.float32)

        got = lax.fori_loop(0, 4, one, jnp.zeros((rows, PARTS[j]), jnp.float32))
        got = (got * factor).astype(jnp.bfloat16)
        if s == 0:
            grecv[j][a] = got
        else:
            gsend[j][s] = got
            send(gsend[j].at[s], grecv[j].at[a], gs_sem.at[j, s], gr_sem.at[j, s], a_dev[4 - s])

    def inner(j):
        for s in (1, 2, 3):
            arrived(grecv[j].at[off(a, s)], gr_sem.at[j, s])

        def one(i, carry):
            span = pl.ds(pl.multiple_of(i * TILE, TILE), TILE)
            for q in range(4):
                where = pl.ds(q * quarter + STARTS[j], PARTS[j])
                gradient = grecv[j][q, span].astype(jnp.float32)
                new_first = (
                    beta_first * fbuf[span, where].astype(jnp.float32) + (1.0 - beta_first) * gradient
                ).astype(jnp.bfloat16)
                new_second = (
                    beta_second * sbuf[span, where].astype(jnp.float32)
                    + (1.0 - beta_second) * gradient * gradient
                ).astype(jnp.bfloat16)
                out_first[span, where] = new_first
                out_second[span, where] = new_second
                ratio = new_first.astype(jnp.float32) / (jnp.sqrt(new_second.astype(jnp.float32)) + epsilon)
                usend[j][q, span] = ratio.astype(jnp.bfloat16)
            urecv[j][rep, span] = usend[j][rep, span]
            return carry

        lax.fori_loop(0, rows // TILE, one, 0)
        for d in (2, 3, 1):
            send(usend[j].at[off(rep, d)], urecv[j].at[rep], us_sem.at[j, d - 1], ur_sem.at[j, d - 1], r_dev[d])

    def limits():
        for d in (1, 2, 3):
            arrived(ebuf.at[off(rep, -d)], er_sem.at[d - 1])
        loads[5].wait()
        blocks = ebuf.shape[1]
        span_of = lax.broadcasted_iota(jnp.int32, (blocks, quarter), 1) // (quarter // blocks)
        spread = (span_of == lax.broadcasted_iota(jnp.int32, (blocks, quarter), 0)).astype(jnp.float32).astype(jnp.bfloat16)
        for r in range(4):
            level = (clip_limit * jnp.exp2(ebuf[r].astype(jnp.float32))).astype(jnp.bfloat16)
            limbuf[r] = lax.dot_general(
                level, spread, (((0,), (0,)), ((), ())), preferred_element_type=jnp.float32
            ).astype(jnp.bfloat16)

    def outer(j):
        for d in (1, 2, 3):
            arrived(urecv[j].at[off(rep, -d)], ur_sem.at[j, d - 1])

        def one(i, carry):
            span = pl.ds(pl.multiple_of(i * TILE, TILE), TILE)
            where = pl.ds(STARTS[j], PARTS[j])
            weight = wbuf[span, where].astype(jnp.float32)
            total = jnp.zeros_like(weight)
            for r in range(4):
                delta = inner_rate * (urecv[j][r, span].astype(jnp.float32) + decay_rate * weight)
                limit = limbuf[r, span, where].astype(jnp.float32)
                total = total + jnp.minimum(jnp.maximum(delta, -limit), limit)
            pseudo = total * 0.25
            new_mom = outer_beta * mbuf[span, where] + pseudo
            out_mom[span, where] = new_mom
            out_weight[span, where] = (weight - outer_rate * (pseudo + outer_beta * new_mom)).astype(jnp.bfloat16)
            return carry

        lax.fori_loop(0, rows // TILE, one, 0)

    def moments():
        for copy in loads[1:5]:
            copy.wait()

    act_out(0)
    act_out(1)
    act_out(2)
    act_out(3)
    cot_out(0)
    z_one(1)
    cot_out(1)
    z_one(3)
    z_one(2)
    cot_one(0)
    b_one(3, 0)
    z_two(3)
    b_one(3, 1)
    cot_one(1)
    b_one(3, 2)
    z_two(2)
    z_one(0)
    b_one(2, 2)
    b_one(2, 1)
    limits()
    b_one(2, 0)
    z_three(3)
    cot_two()
    b_two(3, 2)
    b_one(3, 3)
    z_two(1)
    b_two(2, 1)
    z_three(2)
    b_one(1, 1)
    b_two(3, 0)
    b_one(2, 3)
    b_two(3, 1)
    b_two(2, 2)
    b_two(3, 3)
    b_one(1, 2)
    z_two(0)
    b_two(2, 0)
    b_one(0, 2)
    b_one(1, 0)
    b_three(3)
    b_one(0, 1)
    loads[0].wait()
    product(3, 1)
    z_three(1)
    cot_three()
    b_two(1, 1)
    b_one(1, 3)
    b_two(2, 3)
    product(3, 0)
    product(3, 3)
    b_two(1, 2)
    z_three(0)
    b_two(1, 0)
    product(3, 2)
    b_one(0, 3)
    b_two(1, 3)
    b_one(0, 0)
    b_three(2)
    product(2, 3)
    product(2, 0)
    product(2, 1)
    b_two(0, 2)
    product(2, 2)
    moments()
    inner(3)
    b_two(0, 1)
    b_three(1)
    b_two(0, 3)
    product(1, 3)
    product(1, 0)
    b_two(0, 0)
    product(1, 2)
    product(1, 1)
    inner(2)
    b_three(0)
    product(0, 3)
    product(0, 1)
    product(0, 2)
    inner(1)
    product(0, 0)
    inner(0)
    outer(3)
    outer(2)
    outer(1)
    outer(0)
    for copy in pending:
        copy.wait_send()


def flush(*refs):
    count = (len(refs) - 1) // 2
    sem = refs[-1]
    copies = [pltpu.make_async_copy(refs[i], refs[count + i], sem.at[i]) for i in range(count)]
    for copy in copies:
        copy.start()
    for copy in copies:
        copy.wait()


def expo_own(expo, q):
    blocks = expo.shape[0] // 4
    return expo.at[pl.ds(pl.multiple_of(q * blocks, blocks), blocks)]


def shards(activations, cotangent, weight, first_moment, second_moment, momentum, exponents):
    act, cot, first, second = activations[0], cotangent[0], first_moment[0], second_moment[0]
    expo = exponents[0].T
    rows, width = first.shape
    count, tokens = act.shape[0], cot.shape[1]
    quarter = weight.shape[1]
    bf16, f32 = jnp.bfloat16, jnp.float32
    dma = pltpu.SemaphoreType.DMA
    results = (
        (weight.shape, bf16),
        (momentum.shape, f32),
        (first.shape, bf16),
        (second.shape, bf16),
    )
    pieces = [pltpu.VMEM((4, rows, part), bf16) for part in PARTS]
    held = pl.pallas_call(
        kernel,
        out_shape=tuple(pltpu.VMEM(*r) for r in results),
        in_specs=[pl.BlockSpec(memory_space=pltpu.HBM)] * 7,
        out_specs=(pl.BlockSpec(memory_space=pltpu.VMEM),) * 4,
        scratch_shapes=[
            pltpu.VMEM((4, rows, tokens), bf16),
            [pltpu.VMEM((4, 4, 4, count, part), bf16) for part in PARTS],
            pltpu.VMEM((rows, width), bf16),
            pltpu.VMEM((rows, width), bf16),
            pltpu.VMEM((rows, quarter), bf16),
            pltpu.VMEM((rows, quarter), f32),
            pieces, pieces, pieces, pieces,
            pltpu.VMEM((4, expo.shape[0] // 4, rows), jnp.int32),
            pltpu.VMEM((4, rows, quarter), bf16),
            dma((6,)), dma((CHUNKS,)),
            dma((6,)), dma((6,)),
            dma((CHUNKS, 3)), dma((CHUNKS, 3)),
            dma((CHUNKS, 3)), dma((CHUNKS, 3)),
            dma((CHUNKS, 3, 4)), dma((CHUNKS, 3, 4)),
            dma((CHUNKS, 4)), dma((CHUNKS, 4)),
            dma((CHUNKS, 3)), dma((CHUNKS, 3)),
            dma((3,)), dma((3,)),
        ],
        compiler_params=pltpu.CompilerParams(
            collective_id=0, has_side_effects=True, vmem_limit_bytes=40 * 1024 * 1024
        ),
        cost_estimate=pl.CostEstimate(
            flops=2 * rows * tokens * width, bytes_accessed=14_000_000, transcendentals=rows * width
        ),
    )(*(pltpu.with_memory_space_constraint(v, pltpu.HBM) for v in (act, cot, weight, first, second, momentum, expo)))
    new_weight, new_mom, new_first, new_second = pl.pallas_call(
        flush,
        out_shape=tuple(jax.ShapeDtypeStruct(*r) for r in results),
        in_specs=[pl.BlockSpec(memory_space=pltpu.VMEM)] * 4,
        out_specs=(pl.BlockSpec(memory_space=pltpu.HBM),) * 4,
        scratch_shapes=[dma((4,))],
        compiler_params=pltpu.CompilerParams(vmem_limit_bytes=2 * 1024 * 1024),
    )(*(pltpu.with_memory_space_constraint(v, pltpu.VMEM) for v in held))
    return (new_weight, new_mom, new_first[None], new_second[None])


def solution(mesh):
    in_specs = (
        P("rep", "fsdp", None),
        P("rep", "fsdp", None),
        P("fsdp", "rep"),
        P("rep", "fsdp", None),
        P("rep", "fsdp", None),
        P("fsdp", "rep"),
        P("rep", "fsdp", None),
    )
    out_specs = (P("fsdp", "rep"), P("fsdp", "rep"), P("rep", "fsdp", None), P("rep", "fsdp", None))
    return jax.shard_map(shards, mesh=mesh, in_specs=in_specs, out_specs=out_specs, check_vma=False)
```
